32 devices in a mesh: groups: 2 (over y), dp: 8 (over z, x), tensor: 2 (over core).
Axes of the slice: x: 2, y: 2, z: 4, core: 2. Of those that a mesh axis runs over, the one named last changes fastest.
Arguments:
- train_inputs: bfloat16 [64, 32, 14336], P(('groups', 'dp'), None, 'tensor'), parts along dimension 0, may hold values from -6 to 6
- train_grads: bfloat16 [64, 32, 8192], P(('groups', 'dp'), None, 'tensor'), parts along dimension 0, may hold values from -6 to 6
- train_lengths: int32 [64], P(('groups', 'dp')), parts along dimension 0, may hold values from 4 to 32
- query_inputs: bfloat16 [48, 32, 14336], P(('groups', 'dp'), None, 'tensor'), parts along dimension 0, may hold values from -6 to 6
- query_grads: bfloat16 [48, 32, 8192], P(('groups', 'dp'), None, 'tensor'), parts along dimension 0, may hold values from -6 to 6
- query_lengths: int32 [48], P(('groups', 'dp')), parts along dimension 0, may hold values from 4 to 32
- proj_in: bfloat16 [2, 64, 7168], P('tensor', None, 'dp'), may hold values from -0.046875 to 0.046875
- proj_out: bfloat16 [2, 64, 4096], P('tensor', None, 'dp'), may hold values from -0.0625 to 0.0625
Outputs:
- scores: float32 [64, 24], P(('groups', 'dp', 'tensor')), parts along dimension 0
The draws below stay inside these ranges and needn't reach their ends.
There are 2 independent parts, one for each index of `groups`. The reference program is written for one: setup_inputs(seed, part) draws one part's arguments, and reference() takes and returns one part's arrays. A program takes and returns all parts, laid end to end along the dimension named above; an argument that names none is the same for every part. Nothing has to cross between parts.
All inputs are finite; a program needn't handle non-finite values.
Results may differ from the reference program's by a relative error of at most 0.015.
Values may be sent and summed in bfloat16 or wider, within the bound.
A program may use at most 64 MiB of HBM per device.

```python
import jax
import jax.numpy as jnp
from jax import lax

D = 8192
HID = 14336
RANK = 64
SEQ = 32
TRAIN = 32
QUERIES = 24
N_TENSOR = 2


def touch_ends(result, own_key, smallest, largest):
    index_at = [jax.random.randint(jax.random.fold_in(own_key, axis), (), 0, length) for axis, length in enumerate(result.shape)]
    longest = result.shape.index(max(result.shape))
    beside = index_at[:longest] + [(index_at[longest] + 1) % result.shape[longest]] + index_at[longest + 1:]
    return result.at[tuple(index_at)].set(smallest).at[tuple(beside)].set(largest)


def shard_levels(rng, shape, cuts, least, top_value):
    def one(axis_at, shards_of):
        heights = jax.random.uniform(jax.random.fold_in(jax.random.fold_in(rng, 6), axis_at), (shards_of,), jnp.float32, least / len(cuts), top_value / len(cuts))
        return jnp.repeat(jnp.exp(heights), shape[axis_at] // shards_of).reshape((-1,) + (1,) * (len(shape) - axis_at - 1))

    level = one(*cuts[0])
    for cut in cuts[1:]:
        level = level * one(*cut)
    return level


def centred(own_key, dims, scale, limit, split=(), kind=jnp.bfloat16):
    factor_of = shard_levels(own_key, dims, split, -0.22, 0.18) if split else 1.0
    array = jax.random.normal(own_key, dims, jnp.float32) * scale * factor_of
    return jnp.minimum(jnp.maximum(array, -limit), limit).astype(kind)


def setup_inputs(seed: int = 0, part: int = 0) -> dict:
    seeds = jax.random.split(jax.random.key(seed), 9)
    part_splits = jax.random.split(jax.random.fold_in(seeds[8], part), 9)
    train_inputs = centred(part_splits[0], (TRAIN, SEQ, HID), 1.0, 6.0, ((0, 8), (2, 2)))
    train_grads = centred(part_splits[1], (TRAIN, SEQ, D), 1.0, 6.0, ((0, 8), (2, 2)))
    train_lengths = touch_ends(jax.random.randint(part_splits[2], (TRAIN,), 4, SEQ + 1), jax.random.fold_in(part_splits[2], 1), 4, SEQ).astype(jnp.int32)
    query_inputs = centred(part_splits[3], (QUERIES, SEQ, HID), 1.0, 6.0, ((0, 8), (2, 2)))
    query_grads = centred(part_splits[4], (QUERIES, SEQ, D), 1.0, 6.0, ((0, 8), (2, 2)))
    query_lengths = touch_ends(jax.random.randint(part_splits[5], (QUERIES,), 4, SEQ + 1), jax.random.fold_in(part_splits[5], 1), 4, SEQ).astype(jnp.int32)
    proj_in = centred(seeds[6], (N_TENSOR, RANK, HID // N_TENSOR), HID ** -0.5, 0.046875, ((0, 2), (2, 8)))
    proj_out = centred(seeds[7], (N_TENSOR, RANK, D // N_TENSOR), D ** -0.5, 0.0625, ((0, 2), (2, 8)))
    return dict(train_inputs=train_inputs, train_grads=train_grads, train_lengths=train_lengths, query_inputs=query_inputs, query_grads=query_grads, query_lengths=query_lengths, proj_in=proj_in, proj_out=proj_out)


def assemble(blocks):
    return jnp.transpose(blocks, (1, 0, 2)).reshape(blocks.shape[1], blocks.shape[0] * blocks.shape[2])


def project_tokens(inputs, grads, proj_in, proj_out):
    count = inputs.shape[0] * inputs.shape[1]
    in_side = lax.dot_general(inputs.reshape(count, inputs.shape[2]), proj_in, (((1,), (1,)), ((), ())), preferred_element_type=jnp.float32)
    out_side = lax.dot_general(grads.reshape(count, grads.shape[2]), proj_out, (((1,), (1,)), ((), ())), preferred_element_type=jnp.float32)
    joined = jnp.concatenate([in_side, out_side], axis=1)
    return joined.reshape(inputs.shape[0], inputs.shape[1], joined.shape[1])


def seq_gradient(projected, lengths):
    proj_rank = projected.shape[2] // 2
    seq_len = projected.shape[1]
    live_weight = (jnp.arange(seq_len, dtype=jnp.int32)[None, :] < lengths[:, None]).astype(jnp.float32) / lengths.astype(jnp.float32)[:, None]
    left_side = projected[:, :, :proj_rank] * live_weight[:, :, None]
    right_side = projected[:, :, proj_rank:]
    outer = jnp.einsum('nsr,nsc->nrc', left_side, right_side)
    return outer.reshape(projected.shape[0], proj_rank * proj_rank).astype(jnp.bfloat16)


def reference(train_inputs, train_grads, train_lengths, query_inputs, query_grads, query_lengths, proj_in, proj_out):
    full_in = assemble(proj_in)
    full_out = assemble(proj_out)
    train_proj = project_tokens(train_inputs, train_grads, full_in, full_out)
    query_proj = project_tokens(query_inputs, query_grads, full_in, full_out)
    train_grad = seq_gradient(train_proj, train_lengths)
    query_grad = seq_gradient(query_proj, query_lengths)
    return lax.dot_general(train_grad, query_grad, (((1,), (1,)), ((), ())), preferred_element_type=jnp.float32)
```

```python
import functools

import jax
import jax.numpy as jnp
from jax import lax
from jax.experimental import pallas as pl
from jax.experimental.pallas import tpu as pltpu
from jax.sharding import PartitionSpec as P

MESH = pl.DeviceIdType.MESH
F32 = jnp.float32
BF16 = jnp.bfloat16


def project_tokens(inputs, grads, proj_in, proj_out):
    count = inputs.shape[0] * inputs.shape[1]
    in_side = lax.dot_general(
        inputs.reshape(count, inputs.shape[2]),
        proj_in,
        (((1,), (1,)), ((), ())),
        preferred_element_type=jnp.float32,
    )
    out_side = lax.dot_general(
        grads.reshape(count, grads.shape[2]),
        proj_out,
        (((1,), (1,)), ((), ())),
        preferred_element_type=jnp.float32,
    )
    joined = jnp.concatenate([in_side, out_side], axis=1)
    return joined.reshape(inputs.shape[0], inputs.shape[1], joined.shape[1])


def seq_gradient(projected, lengths, row_count):
    proj_rank = projected.shape[2] // 2
    seq_len = projected.shape[1]
    live_weight = (jnp.arange(seq_len, dtype=jnp.int32)[None, :] < lengths[:, None]).astype(
        jnp.float32
    ) / lengths.astype(jnp.float32)[:, None]
    left_side = projected[:, :, :proj_rank] * live_weight[:, :, None]
    right_side = projected[:, :, proj_rank:]
    outer = jnp.einsum("nsr,nsc->nrc", left_side, right_side)
    return outer.reshape(projected.shape[0], row_count * proj_rank).astype(jnp.bfloat16)


def pair_scores(train_grad, block):
    return lax.dot_general(
        train_grad, block, (((1,), (1,)), ((), ())), preferred_element_type=jnp.float32
    )


def score_against(train_grad, query_grad):
    return pair_scores(train_grad, lax.all_gather(query_grad, "dp", axis=0, tiled=True))


def any_mesh(
    train_inputs,
    train_grads,
    train_lengths,
    query_inputs,
    query_grads,
    query_lengths,
    proj_in,
    proj_out,
):
    whole_in, whole_out = (
        lax.all_gather(proj_in, "dp", axis=2, tiled=True),
        lax.all_gather(proj_out, "dp", axis=2, tiled=True),
    )
    half_in = whole_in[0]
    half_out = whole_out[0]
    train_part = project_tokens(train_inputs, train_grads, half_in, half_out)
    query_part = project_tokens(query_inputs, query_grads, half_in, half_out)
    proj_rank = half_in.shape[0]
    share_rows = train_inputs.shape[0] // lax.axis_size("tensor")
    core_index = lax.axis_index("tensor")
    own_lengths = lax.dynamic_slice_in_dim(train_lengths, core_index * share_rows, share_rows, 0)
    train_proj, query_proj = lax.psum((train_part, query_part), "tensor")
    own_proj = lax.dynamic_slice_in_dim(train_proj, core_index * share_rows, share_rows, 0)
    query_grad = seq_gradient(query_proj, query_lengths, proj_rank)
    return score_against(seq_gradient(own_proj, own_lengths, proj_rank), query_grad)


NT = (((1,), (1,)), ((), ()))
TN = (((0,), (0,)), ((), ()))


def fused_kernel(
    cfg,
    xt_hbm, gt_hbm, lt_ref, xq_hbm, gq_hbm, lq_ref, pin_hbm, pout_hbm,
    out_ref,
    x_all, g_all, p_all, acc_a, acc_b, part, other, q_all, t_grad,
    load_sem, own_sem, z_send, z_recv, x_send, x_recv, y_send, y_recv,
    c_send, c_recv, q_send, q_recv,
):
    n_train, n_query, seq, rank, cin, cout, n_dp = cfg
    n_z = n_dp // 2
    rows_t, rows_q = n_train * seq, n_query * seq
    half = rank // 2
    own_t = n_train // 2

    g = lax.axis_index("groups")
    d = lax.axis_index("dp")
    core = lax.axis_index("tensor")
    z, x = d // 2, d % 2

    own = [
        pltpu.make_async_copy(pin_hbm, p_all.at[d, :, pl.ds(0, cin)], own_sem.at[0]),
        pltpu.make_async_copy(pout_hbm, p_all.at[d, :, pl.ds(cin, cout)], own_sem.at[1]),
    ]
    loads = [
        pltpu.make_async_copy(xt_hbm, x_all.at[pl.ds(0, rows_t)], load_sem.at[0]),
        pltpu.make_async_copy(gt_hbm, g_all.at[pl.ds(0, rows_t)], load_sem.at[1]),
        pltpu.make_async_copy(xq_hbm, x_all.at[pl.ds(rows_t, rows_q)], load_sem.at[2]),
        pltpu.make_async_copy(gq_hbm, g_all.at[pl.ds(rows_t, rows_q)], load_sem.at[3]),
    ]
    for c in own + loads:
        c.start()

    barrier = pltpu.get_barrier_semaphore()
    for k in range(1, n_dp):
        pl.semaphore_signal(
            barrier, inc=1, device_id={"dp": lax.rem(d + k, n_dp)}, device_id_type=MESH
        )
    pl.semaphore_signal(barrier, inc=1, device_id={"tensor": 1 - core}, device_id_type=MESH)
    pl.semaphore_signal(barrier, inc=1, device_id={"groups": 1 - g}, device_id_type=MESH)
    for c in own:
        c.wait()
    pl.semaphore_wait(barrier, n_dp + 1)

    up = z // 2
    m = z + up * (n_z - 1 - 2 * z)

    def mirror(v):
        return v + up * (n_z - 1 - 2 * v)

    def z_copy(zb, zt, lane):
        blk = p_all.at[zb * 2 + x]
        return pltpu.make_async_remote_copy(
            src_ref=blk, dst_ref=blk, send_sem=z_send.at[lane], recv_sem=z_recv.at[zb],
            device_id={"dp": zt * 2 + x}, device_id_type=MESH,
        )

    def x_copy(zb, src_x):
        blk = p_all.at[zb * 2 + src_x, pl.ds(g * half, half)]
        return pltpu.make_async_remote_copy(
            src_ref=blk, dst_ref=blk, send_sem=x_send.at[zb], recv_sem=x_recv.at[zb],
            device_id={"dp": z * 2 + 1 - x}, device_id_type=MESH,
        )

    def y_copy(zb, src_g):
        blk = p_all.at[zb * 2 + 1 - x, pl.ds(src_g * half, half)]
        return pltpu.make_async_remote_copy(
            src_ref=blk, dst_ref=blk, send_sem=y_send.at[zb], recv_sem=y_recv.at[zb],
            device_id={"groups": 1 - g}, device_id_type=MESH,
        )

    zbs = [mirror(1 - m), mirror(2), mirror(3)]
    hops = [mirror(2), mirror(0), mirror(0)]
    first = mirror(1 - m)
    inside = m == 1

    sends = [z_copy(z, first, 0)]
    sends[0].start()
    inner = [z_copy(z, mirror(2), 1)]

    @pl.when(inside)
    def _():
        inner[0].start()

    xs = [x_copy(z, x)]
    xs[0].start()
    for c in loads:
        c.wait()

    def dots(block, start):
        cols_in = pl.ds(pl.multiple_of(block * cin, 128), cin)
        cols_out = pl.ds(pl.multiple_of(block * cout, 128), cout)
        a = lax.dot_general(
            x_all[:, cols_in], p_all[block, :, 0:cin], NT, preferred_element_type=F32
        )
        b = lax.dot_general(
            g_all[:, cols_out], p_all[block, :, cin:cin + cout], NT, preferred_element_type=F32
        )
        if start:
            acc_a[...] = a
            acc_b[...] = b
        else:
            acc_a[...] += a
            acc_b[...] += b

    dots(d, True)

    order = [z] + zbs
    ys = []
    for k in range(n_z):
        if k < n_z - 1:
            zb = zbs[k]
            z_copy(zb, first, 0).wait_recv()
            hop = z_copy(zb, hops[k], 2 + k)
            inner.append(hop)

            @pl.when(inside)
            def _(hop=hop):
                hop.start()

            c = x_copy(zb, x)
            c.start()
            xs.append(c)
        x_copy(order[k], 1 - x).wait_recv()
        c = y_copy(order[k], g)
        c.start()
        ys.append(c)
        if k < n_z - 1:
            dots(zbs[k] * 2 + x, False)
        y_copy(order[k], 1 - g).wait_recv()
        dots(order[k] * 2 + 1 - x, False)

    part[:, 0:rank] = acc_a[...]
    part[:, rank:2 * rank] = acc_b[...]

    mine = core * (own_t * seq)
    theirs = (1 - core) * (own_t * seq)
    cq = pltpu.make_async_remote_copy(
        src_ref=part.at[pl.ds(rows_t, rows_q)], dst_ref=other.at[pl.ds(own_t * seq, rows_q)],
        send_sem=c_send.at[0], recv_sem=c_recv.at[0],
        device_id={"tensor": 1 - core}, device_id_type=MESH,
    )
    ct = pltpu.make_async_remote_copy(
        src_ref=part.at[pl.ds(theirs, own_t * seq)], dst_ref=other.at[pl.ds(0, own_t * seq)],
        send_sem=c_send.at[1], recv_sem=c_recv.at[1],
        device_id={"tensor": 1 - core}, device_id_type=MESH,
    )
    cq.start()
    ct.start()

    step = lax.broadcasted_iota(jnp.int32, (seq, rank), 0)

    def gradient(total, length):
        size = jnp.broadcast_to(length, (seq, rank))
        weight = jnp.where(step < size, 1.0, 0.0) / size.astype(F32)
        a = total[:, 0:rank] * weight
        b = total[:, rank:2 * rank]
        h = lax.dot_general(
            a, b, TN, preferred_element_type=F32, precision=lax.Precision.HIGHEST
        ).astype(BF16)
        return jnp.concatenate([h[0:half], h[half:rank]], axis=1)

    cq.wait_recv()
    for i in range(n_query):
        lo = rows_t + i * seq
        total = part[lo:lo + seq] + other[own_t * seq + i * seq:own_t * seq + (i + 1) * seq]
        q_all[d, i * half:(i + 1) * half] = gradient(total, lq_ref[i])
    qs = []
    for k in range(1, n_dp):
        c = pltpu.make_async_remote_copy(
            src_ref=q_all.at[d], dst_ref=q_all.at[d],
            send_sem=q_send.at[k], recv_sem=q_recv.at[d],
            device_id={"dp": lax.rem(d + k, n_dp)}, device_id_type=MESH,
        )
        c.start()
        qs.append(c)
    ct.wait_recv()
    for i in range(own_t):
        total = part[pl.ds(mine + i * seq, seq)] + other[i * seq:(i + 1) * seq]
        t_grad[i * half:(i + 1) * half] = gradient(total, lt_ref[core * own_t + i])

    for k in range(1, n_dp):
        src = lax.rem(d + k, n_dp)
        blk = q_all.at[src]
        pltpu.make_async_remote_copy(
            src_ref=blk, dst_ref=blk, send_sem=q_send.at[k], recv_sem=q_recv.at[src],
            device_id={"dp": src}, device_id_type=MESH,
        ).wait_recv()

    width = own_t * half
    queries = n_dp * n_query
    q_flat = q_all[...].reshape(queries * half, 2 * rank)
    pairs = lax.dot_general(q_flat, t_grad[...], NT, preferred_element_type=F32)
    pairs = pairs.reshape(queries, half, width)
    row = lax.broadcasted_iota(jnp.int32, (queries, half, width), 1)
    col = lax.broadcasted_iota(jnp.int32, (queries, half, width), 2) % half
    diag = jnp.sum(jnp.where(row == col, pairs, 0.0), axis=1)
    pick = (
        lax.broadcasted_iota(jnp.int32, (own_t, width), 1) // half
        == lax.broadcasted_iota(jnp.int32, (own_t, width), 0)
    ).astype(F32)
    out_ref[...] = lax.dot_general(
        pick, diag, NT, preferred_element_type=F32, precision=lax.Precision.HIGHEST
    )

    for c in sends + xs + ys + [cq, ct] + qs:
        c.wait_send()

    @pl.when(inside)
    def _():
        for c in inner:
            c.wait_send()


def fused(
    train_inputs, train_grads, train_lengths, query_inputs, query_grads, query_lengths,
    proj_in, proj_out,
):
    n_dp = lax.axis_size("dp")
    n_train, seq, win = train_inputs.shape
    n_query, _, wout = query_grads.shape
    _, rank, cin = proj_in.shape
    cout = proj_out.shape[2]
    rows_t, rows_q = n_train * seq, n_query * seq
    rows = rows_t + rows_q
    half = rank // 2
    own_t = n_train // 2
    cfg = (n_train, n_query, seq, rank, cin, cout, n_dp)
    hbm = pl.BlockSpec(memory_space=pl.ANY)
    smem = pl.BlockSpec(memory_space=pltpu.SMEM)
    dma = pltpu.SemaphoreType.DMA
    return pl.pallas_call(
        functools.partial(fused_kernel, cfg),
        out_shape=jax.ShapeDtypeStruct((own_t, n_dp * n_query), F32),
        in_specs=[hbm, hbm, smem, hbm, hbm, smem, hbm, hbm],
        out_specs=pl.BlockSpec(memory_space=pltpu.VMEM),
        scratch_shapes=[
            pltpu.VMEM((rows, win), BF16),
            pltpu.VMEM((rows, wout), BF16),
            pltpu.VMEM((n_dp, rank, cin + cout), BF16),
            pltpu.VMEM((rows, rank), F32),
            pltpu.VMEM((rows, rank), F32),
            pltpu.VMEM((rows, 2 * rank), F32),
            pltpu.VMEM((own_t * seq + rows_q, 2 * rank), F32),
            pltpu.VMEM((n_dp, n_query * half, 2 * rank), BF16),
            pltpu.VMEM((own_t * half, 2 * rank), BF16),
            dma((4,)),
            dma((2,)),
            dma((5,)),
            dma((4,)),
            dma((4,)),
            dma((4,)),
            dma((4,)),
            dma((4,)),
            dma((2,)),
            dma((2,)),
            dma((n_dp,)),
            dma((n_dp,)),
        ],
        compiler_params=pltpu.CompilerParams(
            collective_id=0, has_side_effects=True, vmem_limit_bytes=40 * 1024 * 1024
        ),
    )(
        train_inputs.reshape(rows_t, win),
        train_grads.reshape(rows_t, wout),
        train_lengths,
        query_inputs.reshape(rows_q, win),
        query_grads.reshape(rows_q, wout),
        query_lengths,
        proj_in[0],
        proj_out[0],
    )


def per_device(*args):
    proj_in, proj_out = args[6], args[7]
    sizes = (lax.axis_size("groups"), lax.axis_size("dp"), lax.axis_size("tensor"))
    fits = (
        sizes == (2, 8, 2)
        and proj_in.shape[2] % 128 == 0
        and proj_out.shape[2] % 128 == 0
        and proj_in.shape[1] == 64
        and args[0].shape[0] % 2 == 0
        and args[0].shape[1] % 16 == 0
    )
    return fused(*args) if fits else any_mesh(*args)


def solution(mesh):
    return jax.shard_map(
        per_device,
        mesh=mesh,
        in_specs=(
            P(("groups", "dp"), None, "tensor"),
            P(("groups", "dp"), None, "tensor"),
            P(("groups", "dp")),
            P(("groups", "dp"), None, "tensor"),
            P(("groups", "dp"), None, "tensor"),
            P(("groups", "dp")),
            P("tensor", None, "dp"),
            P("tensor", None, "dp"),
        ),
        out_specs=P(("groups", "dp", "tensor"), None),
        check_vma=False,
    )
```

```python
import functools

import jax
import jax.numpy as jnp
from jax import lax
from jax.experimental import pallas as pl
from jax.experimental.pallas import tpu as pltpu
from jax.sharding import PartitionSpec as P

MESH = pl.DeviceIdType.MESH
F32 = jnp.float32
BF16 = jnp.bfloat16


def project_tokens(inputs, grads, proj_in, proj_out):
    count = inputs.shape[0] * inputs.shape[1]
    in_side = lax.dot_general(
        inputs.reshape(count, inputs.shape[2]),
        proj_in,
        (((1,), (1,)), ((), ())),
        preferred_element_type=jnp.float32,
    )
    out_side = lax.dot_general(
        grads.reshape(count, grads.shape[2]),
        proj_out,
        (((1,), (1,)), ((), ())),
        preferred_element_type=jnp.float32,
    )
    joined = jnp.concatenate([in_side, out_side], axis=1)
    return joined.reshape(inputs.shape[0], inputs.shape[1], joined.shape[1])


def seq_gradient(projected, lengths, row_count):
    proj_rank = projected.shape[2] // 2
    seq_len = projected.shape[1]
    live_weight = (jnp.arange(seq_len, dtype=jnp.int32)[None, :] < lengths[:, None]).astype(
        jnp.float32
    ) / lengths.astype(jnp.float32)[:, None]
    left_side = projected[:, :, :proj_rank] * live_weight[:, :, None]
    right_side = projected[:, :, proj_rank:]
    outer = jnp.einsum("nsr,nsc->nrc", left_side, right_side)
    return outer.reshape(projected.shape[0], row_count * proj_rank).astype(jnp.bfloat16)


def pair_scores(train_grad, block):
    return lax.dot_general(
        train_grad, block, (((1,), (1,)), ((), ())), preferred_element_type=jnp.float32
    )


def score_against(train_grad, query_grad):
    return pair_scores(train_grad, lax.all_gather(query_grad, "dp", axis=0, tiled=True))


def any_mesh(
    train_inputs,
    train_grads,
    train_lengths,
    query_inputs,
    query_grads,
    query_lengths,
    proj_in,
    proj_out,
):
    whole_in, whole_out = (
        lax.all_gather(proj_in, "dp", axis=2, tiled=True),
        lax.all_gather(proj_out, "dp", axis=2, tiled=True),
    )
    half_in = whole_in[0]
    half_out = whole_out[0]
    train_part = project_tokens(train_inputs, train_grads, half_in, half_out)
    query_part = project_tokens(query_inputs, query_grads, half_in, half_out)
    proj_rank = half_in.shape[0]
    share_rows = train_inputs.shape[0] // lax.axis_size("tensor")
    core_index = lax.axis_index("tensor")
    own_lengths = lax.dynamic_slice_in_dim(train_lengths, core_index * share_rows, share_rows, 0)
    train_proj, query_proj = lax.psum((train_part, query_part), "tensor")
    own_proj = lax.dynamic_slice_in_dim(train_proj, core_index * share_rows, share_rows, 0)
    query_grad = seq_gradient(query_proj, query_lengths, proj_rank)
    return score_against(seq_gradient(own_proj, own_lengths, proj_rank), query_grad)


NT = (((1,), (1,)), ((), ()))
TN = (((0,), (0,)), ((), ()))


def fused_kernel(
    cfg,
    xt_hbm, gt_hbm, lt_hbm, xq_hbm, gq_hbm, lq_hbm, pin_hbm, pout_hbm,
    out_ref,
    lt_ref, lq_ref, x_all, g_all, p_all, acc_a, acc_b, part, other, q_all, t_grad,
    load_sem, own_sem, z_send, z_recv, x_send, x_recv, y_send, y_recv,
    c_send, c_recv, q_send, q_recv,
):
    n_train, n_query, seq, rank, cin, cout, n_dp = cfg
    n_z = n_dp // 2
    rows_t, rows_q = n_train * seq, n_query * seq
    half = rank // 2
    own_t = n_train // 2

    g = lax.axis_index("groups")
    d = lax.axis_index("dp")
    core = lax.axis_index("tensor")
    z, x = d // 2, d % 2

    own = [
        pltpu.make_async_copy(pin_hbm, p_all.at[d, :, pl.ds(0, cin)], own_sem.at[0]),
        pltpu.make_async_copy(pout_hbm, p_all.at[d, :, pl.ds(cin, cout)], own_sem.at[1]),
    ]
    loads = [
        pltpu.make_async_copy(xt_hbm, x_all.at[pl.ds(0, rows_t)], load_sem.at[0]),
        pltpu.make_async_copy(gt_hbm, g_all.at[pl.ds(0, rows_t)], load_sem.at[1]),
        pltpu.make_async_copy(xq_hbm, x_all.at[pl.ds(rows_t, rows_q)], load_sem.at[2]),
        pltpu.make_async_copy(gq_hbm, g_all.at[pl.ds(rows_t, rows_q)], load_sem.at[3]),
        pltpu.make_async_copy(lt_hbm, lt_ref, load_sem.at[4]),
        pltpu.make_async_copy(lq_hbm, lq_ref, load_sem.at[5]),
    ]
    for c in own + loads:
        c.start()

    barrier = pltpu.get_barrier_semaphore()
    for k in range(1, n_dp):
        pl.semaphore_signal(
            barrier, inc=1, device_id={"dp": lax.rem(d + k, n_dp)}, device_id_type=MESH
        )
    pl.semaphore_signal(barrier, inc=1, device_id={"tensor": 1 - core}, device_id_type=MESH)
    pl.semaphore_signal(barrier, inc=1, device_id={"groups": 1 - g}, device_id_type=MESH)
    for c in own:
        c.wait()
    pl.semaphore_wait(barrier, n_dp + 1)

    up = z // 2
    m = z + up * (n_z - 1 - 2 * z)

    def mirror(v):
        return v + up * (n_z - 1 - 2 * v)

    def z_copy(zb, zt, part_no, lane):
        rows = (g if part_no == 0 else 1 - g) * half
        blk = p_all.at[zb * 2 + x, pl.ds(rows, half)]
        return pltpu.make_async_remote_copy(
            src_ref=blk, dst_ref=blk,
            send_sem=z_send.at[2 * lane + part_no], recv_sem=z_recv.at[2 * zb + part_no],
            device_id={"dp": zt * 2 + x}, device_id_type=MESH,
        )

    def x_copy(zb, src_x):
        blk = p_all.at[zb * 2 + src_x, pl.ds(g * half, half)]
        return pltpu.make_async_remote_copy(
            src_ref=blk, dst_ref=blk, send_sem=x_send.at[zb], recv_sem=x_recv.at[zb],
            device_id={"dp": z * 2 + 1 - x}, device_id_type=MESH,
        )

    def y_copy(zb, src_g):
        blk = p_all.at[zb * 2 + 1 - x, pl.ds(src_g * half, half)]
        return pltpu.make_async_remote_copy(
            src_ref=blk, dst_ref=blk, send_sem=y_send.at[zb], recv_sem=y_recv.at[zb],
            device_id={"groups": 1 - g}, device_id_type=MESH,
        )

    zbs = [mirror(1 - m), mirror(2), mirror(3)]
    hops = [mirror(2), mirror(0), mirror(0)]
    first = mirror(1 - m)
    inside = m == 1

    sends, inner, xs, ys = [], [], [], []

    def send_inner(copy):
        inner.append(copy)

        @pl.when(inside)
        def _():
            copy.start()

    for part_no in range(2):
        c = z_copy(z, first, part_no, 0)
        c.start()
        sends.append(c)
        send_inner(z_copy(z, mirror(2), part_no, 1))
        if part_no == 0:
            xs.append(x_copy(z, x))
            xs[0].start()
    for c in loads:
        c.wait()

    def dots(block, start):
        cols_in = pl.ds(pl.multiple_of(block * cin, 128), cin)
        cols_out = pl.ds(pl.multiple_of(block * cout, 128), cout)
        a = lax.dot_general(
            x_all[:, cols_in], p_all[block, :, 0:cin], NT, preferred_element_type=F32
        )
        b = lax.dot_general(
            g_all[:, cols_out], p_all[block, :, cin:cin + cout], NT, preferred_element_type=F32
        )
        if start:
            acc_a[...] = a
            acc_b[...] = b
        else:
            acc_a[...] += a
            acc_b[...] += b

    dots(d, True)

    order = [z] + zbs

    def hand_on(k):
        x_copy(order[k], 1 - x).wait_recv()
        c = y_copy(order[k], g)
        c.start()
        ys.append(c)

    def finish(k):
        y_copy(order[k], 1 - g).wait_recv()
        dots(order[k] * 2 + 1 - x, False)

    for k in range(n_z - 1):
        zb = zbs[k]
        z_copy(zb, first, 0, 0).wait_recv()
        send_inner(z_copy(zb, hops[k], 0, 2 + k))
        c = x_copy(zb, x)
        c.start()
        xs.append(c)
        hand_on(k)
        z_copy(zb, first, 1, 0).wait_recv()
        send_inner(z_copy(zb, hops[k], 1, 2 + k))
        dots(zb * 2 + x, False)
        if k >= 1:
            finish(k - 1)
    hand_on(n_z - 1)
    finish(n_z - 2)
    finish(n_z - 1)

    part[:, 0:rank] = acc_a[...]
    part[:, rank:2 * rank] = acc_b[...]

    mine = core * (own_t * seq)
    theirs = (1 - core) * (own_t * seq)
    cq = pltpu.make_async_remote_copy(
        src_ref=part.at[pl.ds(rows_t, rows_q)], dst_ref=other.at[pl.ds(own_t * seq, rows_q)],
        send_sem=c_send.at[0], recv_sem=c_recv.at[0],
        device_id={"tensor": 1 - core}, device_id_type=MESH,
    )
    ct = pltpu.make_async_remote_copy(
        src_ref=part.at[pl.ds(theirs, own_t * seq)], dst_ref=other.at[pl.ds(0, own_t * seq)],
        send_sem=c_send.at[1], recv_sem=c_recv.at[1],
        device_id={"tensor": 1 - core}, device_id_type=MESH,
    )
    cq.start()
    ct.start()

    step = lax.broadcasted_iota(jnp.int32, (seq, rank), 0)

    def gradient(total, length):
        size = jnp.broadcast_to(length, (seq, rank))
        weight = jnp.where(step < size, 1.0, 0.0) / size.astype(F32)
        a = total[:, 0:rank] * weight
        b = total[:, rank:2 * rank]
        h = lax.dot_general(
            a, b, TN, preferred_element_type=F32, precision=lax.Precision.HIGHEST
        ).astype(BF16)
        return jnp.concatenate([h[0:half], h[half:rank]], axis=1)

    cq.wait_recv()
    for i in range(n_query):
        lo = rows_t + i * seq
        total = part[lo:lo + seq] + other[own_t * seq + i * seq:own_t * seq + (i + 1) * seq]
        q_all[d, i * half:(i + 1) * half] = gradient(total, lq_ref[i])
    qs = []
    for k in range(1, n_dp):
        c = pltpu.make_async_remote_copy(
            src_ref=q_all.at[d], dst_ref=q_all.at[d],
            send_sem=q_send.at[k], recv_sem=q_recv.at[d],
            device_id={"dp": lax.rem(d + k, n_dp)}, device_id_type=MESH,
        )
        c.start()
        qs.append(c)
    ct.wait_recv()
    for i in range(own_t):
        total = part[pl.ds(mine + i * seq, seq)] + other[i * seq:(i + 1) * seq]
        t_grad[i * half:(i + 1) * half] = gradient(total, lt_ref[core * own_t + i])

    for k in range(1, n_dp):
        src = lax.rem(d + k, n_dp)
        blk = q_all.at[src]
        pltpu.make_async_remote_copy(
            src_ref=blk, dst_ref=blk, send_sem=q_send.at[k], recv_sem=q_recv.at[src],
            device_id={"dp": src}, device_id_type=MESH,
        ).wait_recv()

    width = own_t * half
    queries = n_dp * n_query
    q_flat = q_all[...].reshape(queries * half, 2 * rank)
    pairs = lax.dot_general(q_flat, t_grad[...], NT, preferred_element_type=F32)
    pairs = pairs.reshape(queries, half, width)
    row = lax.broadcasted_iota(jnp.int32, (queries, half, width), 1)
    col = lax.broadcasted_iota(jnp.int32, (queries, half, width), 2) % half
    diag = jnp.sum(jnp.where(row == col, pairs, 0.0), axis=1)
    pick = (
        lax.broadcasted_iota(jnp.int32, (own_t, width), 1) // half
        == lax.broadcasted_iota(jnp.int32, (own_t, width), 0)
    ).astype(F32)
    out_ref[...] = lax.dot_general(
        pick, diag, NT, preferred_element_type=F32, precision=lax.Precision.HIGHEST
    )

    for c in sends + xs + ys + [cq, ct] + qs:
        c.wait_send()

    @pl.when(inside)
    def _():
        for c in inner:
            c.wait_send()


def fused(
    train_inputs, train_grads, train_lengths, query_inputs, query_grads, query_lengths,
    proj_in, proj_out,
):
    n_dp = lax.axis_size("dp")
    n_train, seq, win = train_inputs.shape
    n_query, _, wout = query_grads.shape
    _, rank, cin = proj_in.shape
    cout = proj_out.shape[2]
    rows_t, rows_q = n_train * seq, n_query * seq
    rows = rows_t + rows_q
    half = rank // 2
    own_t = n_train // 2
    cfg = (n_train, n_query, seq, rank, cin, cout, n_dp)
    hbm = pl.BlockSpec(memory_space=pltpu.HBM)
    dma = pltpu.SemaphoreType.DMA
    return pl.pallas_call(
        functools.partial(fused_kernel, cfg),
        out_shape=jax.ShapeDtypeStruct((own_t, n_dp * n_query), F32),
        in_specs=[hbm] * 8,
        out_specs=pl.BlockSpec(memory_space=pltpu.VMEM),
        scratch_shapes=[
            pltpu.SMEM((n_train,), jnp.int32),
            pltpu.SMEM((n_query,), jnp.int32),
            pltpu.VMEM((rows, win), BF16),
            pltpu.VMEM((rows, wout), BF16),
            pltpu.VMEM((n_dp, rank, cin + cout), BF16),
            pltpu.VMEM((rows, rank), F32),
            pltpu.VMEM((rows, rank), F32),
            pltpu.VMEM((rows, 2 * rank), F32),
            pltpu.VMEM((own_t * seq + rows_q, 2 * rank), F32),
            pltpu.VMEM((n_dp, n_query * half, 2 * rank), BF16),
            pltpu.VMEM((own_t * half, 2 * rank), BF16),
            dma((6,)),
            dma((2,)),
            dma((10,)),
            dma((8,)),
            dma((4,)),
            dma((4,)),
            dma((4,)),
            dma((4,)),
            dma((2,)),
            dma((2,)),
            dma((n_dp,)),
            dma((n_dp,)),
        ],
        compiler_params=pltpu.CompilerParams(
            collective_id=0, has_side_effects=True, vmem_limit_bytes=64 * 1024 * 1024
        ),
    )(
        train_inputs.reshape(rows_t, win),
        train_grads.reshape(rows_t, wout),
        train_lengths,
        query_inputs.reshape(rows_q, win),
        query_grads.reshape(rows_q, wout),
        query_lengths,
        proj_in[0],
        proj_out[0],
    )


def per_device(*args):
    proj_in, proj_out = args[6], args[7]
    sizes = (lax.axis_size("groups"), lax.axis_size("dp"), lax.axis_size("tensor"))
    fits = (
        sizes == (2, 8, 2)
        and proj_in.shape[2] % 128 == 0
        and proj_out.shape[2] % 128 == 0
        and proj_in.shape[1] == 64
        and args[0].shape[0] % 2 == 0
        and args[0].shape[1] % 16 == 0
    )
    return fused(*args) if fits else any_mesh(*args)


def solution(mesh):
    return jax.shard_map(
        per_device,
        mesh=mesh,
        in_specs=(
            P(("groups", "dp"), None, "tensor"),
            P(("groups", "dp"), None, "tensor"),
            P(("groups", "dp")),
            P(("groups", "dp"), None, "tensor"),
            P(("groups", "dp"), None, "tensor"),
            P(("groups", "dp")),
            P("tensor", None, "dp"),
            P("tensor", None, "dp"),
        ),
        out_specs=P(("groups", "dp", "tensor"), None),
        check_vma=False,
    )
```

```python
import functools

import jax
import jax.numpy as jnp
from jax import lax
from jax.experimental import pallas as pl
from jax.experimental.pallas import tpu as pltpu
from jax.sharding import PartitionSpec as P

MESH = pl.DeviceIdType.MESH
F32 = jnp.float32
BF16 = jnp.bfloat16


def project_tokens(inputs, grads, proj_in, proj_out):
    count = inputs.shape[0] * inputs.shape[1]
    in_side = lax.dot_general(
        inputs.reshape(count, inputs.shape[2]),
        proj_in,
        (((1,), (1,)), ((), ())),
        preferred_element_type=jnp.float32,
    )
    out_side = lax.dot_general(
        grads.reshape(count, grads.shape[2]),
        proj_out,
        (((1,), (1,)), ((), ())),
        preferred_element_type=jnp.float32,
    )
    joined = jnp.concatenate([in_side, out_side], axis=1)
    return joined.reshape(inputs.shape[0], inputs.shape[1], joined.shape[1])


def seq_gradient(projected, lengths, row_count):
    proj_rank = projected.shape[2] // 2
    seq_len = projected.shape[1]
    live_weight = (jnp.arange(seq_len, dtype=jnp.int32)[None, :] < lengths[:, None]).astype(
        jnp.float32
    ) / lengths.astype(jnp.float32)[:, None]
    left_side = projected[:, :, :proj_rank] * live_weight[:, :, None]
    right_side = projected[:, :, proj_rank:]
    outer = jnp.einsum("nsr,nsc->nrc", left_side, right_side)
    return outer.reshape(projected.shape[0], row_count * proj_rank).astype(jnp.bfloat16)


def pair_scores(train_grad, block):
    return lax.dot_general(
        train_grad, block, (((1,), (1,)), ((), ())), preferred_element_type=jnp.float32
    )


def score_against(train_grad, query_grad):
    return pair_scores(train_grad, lax.all_gather(query_grad, "dp", axis=0, tiled=True))


def any_mesh(
    train_inputs,
    train_grads,
    train_lengths,
    query_inputs,
    query_grads,
    query_lengths,
    proj_in,
    proj_out,
):
    whole_in, whole_out = (
        lax.all_gather(proj_in, "dp", axis=2, tiled=True),
        lax.all_gather(proj_out, "dp", axis=2, tiled=True),
    )
    half_in = whole_in[0]
    half_out = whole_out[0]
    train_part = project_tokens(train_inputs, train_grads, half_in, half_out)
    query_part = project_tokens(query_inputs, query_grads, half_in, half_out)
    proj_rank = half_in.shape[0]
    share_rows = train_inputs.shape[0] // lax.axis_size("tensor")
    core_index = lax.axis_index("tensor")
    own_lengths = lax.dynamic_slice_in_dim(train_lengths, core_index * share_rows, share_rows, 0)
    train_proj, query_proj = lax.psum((train_part, query_part), "tensor")
    own_proj = lax.dynamic_slice_in_dim(train_proj, core_index * share_rows, share_rows, 0)
    query_grad = seq_gradient(query_proj, query_lengths, proj_rank)
    return score_against(seq_gradient(own_proj, own_lengths, proj_rank), query_grad)


NT = (((1,), (1,)), ((), ()))
TN = (((0,), (0,)), ((), ()))


def fused_kernel(
    cfg,
    xt_hbm, gt_hbm, lt_hbm, xq_hbm, gq_hbm, lq_hbm, pin_hbm, pout_hbm,
    out_ref,
    lt_ref, lq_ref, x_all, g_all, p_all, acc_a, acc_b, part, other, q_all, t_grad,
    load_sem, own_sem, z_send, z_recv, x_send, x_recv, y_send, y_recv,
    c_send, c_recv, q_send, q_recv,
):
    n_train, n_query, seq, rank, cin, cout, n_dp = cfg
    n_z = n_dp // 2
    rows_t, rows_q = n_train * seq, n_query * seq
    half = rank // 2
    own_t = n_train // 2

    g = lax.axis_index("groups")
    d = lax.axis_index("dp")
    core = lax.axis_index("tensor")
    z, x = d // 2, d % 2

    own = [
        pltpu.make_async_copy(pin_hbm, p_all.at[d, :, pl.ds(0, cin)], own_sem.at[0]),
        pltpu.make_async_copy(pout_hbm, p_all.at[d, :, pl.ds(cin, cout)], own_sem.at[1]),
    ]
    loads = [
        pltpu.make_async_copy(xt_hbm, x_all.at[pl.ds(0, rows_t)], load_sem.at[0]),
        pltpu.make_async_copy(gt_hbm, g_all.at[pl.ds(0, rows_t)], load_sem.at[1]),
        pltpu.make_async_copy(xq_hbm, x_all.at[pl.ds(rows_t, rows_q)], load_sem.at[2]),
        pltpu.make_async_copy(gq_hbm, g_all.at[pl.ds(rows_t, rows_q)], load_sem.at[3]),
        pltpu.make_async_copy(lt_hbm, lt_ref, load_sem.at[4]),
        pltpu.make_async_copy(lq_hbm, lq_ref, load_sem.at[5]),
    ]
    for c in own:
        c.start()

    up = z // 2
    m = z + up * (n_z - 1 - 2 * z)

    def mirror(v):
        return v + up * (n_z - 1 - 2 * v)

    first = mirror(1 - m)
    inside = m == 1

    barrier = pltpu.get_barrier_semaphore()
    pl.semaphore_signal(
        barrier, inc=1, device_id={"dp": first * 2 + x}, device_id_type=MESH
    )

    @pl.when(inside)
    def _():
        pl.semaphore_signal(
            barrier, inc=1, device_id={"dp": mirror(2) * 2 + x}, device_id_type=MESH
        )

    pl.semaphore_signal(barrier, inc=1, device_id={"dp": z * 2 + 1 - x}, device_id_type=MESH)
    pl.semaphore_signal(barrier, inc=1, device_id={"tensor": 1 - core}, device_id_type=MESH)
    pl.semaphore_signal(barrier, inc=1, device_id={"groups": 1 - g}, device_id_type=MESH)
    for c in own:
        c.wait()
    for c in loads:
        c.start()
    pl.semaphore_wait(barrier, 4 + m)

    def z_copy(zb, zt, part_no, lane):
        rows = (g if part_no == 0 else 1 - g) * half
        blk = p_all.at[zb * 2 + x, pl.ds(rows, half)]
        return pltpu.make_async_remote_copy(
            src_ref=blk, dst_ref=blk,
            send_sem=z_send.at[2 * lane + part_no], recv_sem=z_recv.at[2 * zb + part_no],
            device_id={"dp": zt * 2 + x}, device_id_type=MESH,
        )

    def x_copy(zb, src_x):
        blk = p_all.at[zb * 2 + src_x, pl.ds(g * half, half)]
        return pltpu.make_async_remote_copy(
            src_ref=blk, dst_ref=blk, send_sem=x_send.at[zb], recv_sem=x_recv.at[zb],
            device_id={"dp": z * 2 + 1 - x}, device_id_type=MESH,
        )

    def y_copy(zb, src_g):
        blk = p_all.at[zb * 2 + 1 - x, pl.ds(src_g * half, half)]
        return pltpu.make_async_remote_copy(
            src_ref=blk, dst_ref=blk, send_sem=y_send.at[zb], recv_sem=y_recv.at[zb],
            device_id={"groups": 1 - g}, device_id_type=MESH,
        )

    zbs = [mirror(1 - m), mirror(2), mirror(3)]
    hops = [mirror(2), mirror(0), mirror(0)]

    sends, inner, xs, ys = [], [], [], []

    def send_inner(copy):
        inner.append(copy)

        @pl.when(inside)
        def _():
            copy.start()

    def send_own(part_no):
        c = z_copy(z, first, part_no, 0)
        c.start()
        sends.append(c)
        send_inner(z_copy(z, mirror(2), part_no, 1))

    send_own(0)
    xs.append(x_copy(z, x))
    xs[0].start()

    def dots(block, start):
        cols_in = pl.ds(pl.multiple_of(block * cin, 128), cin)
        cols_out = pl.ds(pl.multiple_of(block * cout, 128), cout)
        a = lax.dot_general(
            x_all[:, cols_in], p_all[block, :, 0:cin], NT, preferred_element_type=F32
        )
        b = lax.dot_general(
            g_all[:, cols_out], p_all[block, :, cin:cin + cout], NT, preferred_element_type=F32
        )
        if start:
            acc_a[...] = a
            acc_b[...] = b
        else:
            acc_a[...] += a
            acc_b[...] += b

    order = [z] + zbs

    def hand_on(k):
        x_copy(order[k], 1 - x).wait_recv()
        c = y_copy(order[k], g)
        c.start()
        ys.append(c)

    def finish(k):
        y_copy(order[k], 1 - g).wait_recv()
        dots(order[k] * 2 + 1 - x, False)

    for k in range(n_z - 1):
        zb = zbs[k]
        z_copy(zb, first, 0, 0).wait_recv()
        send_inner(z_copy(zb, hops[k], 0, 2 + k))
        c = x_copy(zb, x)
        c.start()
        xs.append(c)
        if k == 0:
            send_own(1)
        hand_on(k)
        if k == 0:
            for c in loads:
                c.wait()
            dots(d, True)
    finish(0)
    for k in range(n_z - 1):
        zb = zbs[k]
        z_copy(zb, first, 1, 0).wait_recv()
        send_inner(z_copy(zb, hops[k], 1, 2 + k))
        if k == 0:
            hand_on(n_z - 1)
        dots(zb * 2 + x, False)
        finish(k + 1)

    part[:, 0:rank] = acc_a[...]
    part[:, rank:2 * rank] = acc_b[...]

    mine = core * (own_t * seq)
    theirs = (1 - core) * (own_t * seq)
    cq = pltpu.make_async_remote_copy(
        src_ref=part.at[pl.ds(rows_t, rows_q)], dst_ref=other.at[pl.ds(own_t * seq, rows_q)],
        send_sem=c_send.at[0], recv_sem=c_recv.at[0],
        device_id={"tensor": 1 - core}, device_id_type=MESH,
    )
    ct = pltpu.make_async_remote_copy(
        src_ref=part.at[pl.ds(theirs, own_t * seq)], dst_ref=other.at[pl.ds(0, own_t * seq)],
        send_sem=c_send.at[1], recv_sem=c_recv.at[1],
        device_id={"tensor": 1 - core}, device_id_type=MESH,
    )
    cq.start()
    ct.start()

    step = lax.broadcasted_iota(jnp.int32, (seq, rank), 0)

    def gradient(total, length):
        size = jnp.broadcast_to(length, (seq, rank))
        weight = jnp.where(step < size, 1.0, 0.0) / size.astype(F32)
        a = total[:, 0:rank] * weight
        b = total[:, rank:2 * rank]
        h = lax.dot_general(
            a, b, TN, preferred_element_type=F32, precision=lax.Precision.HIGHEST
        ).astype(BF16)
        return jnp.concatenate([h[0:half], h[half:rank]], axis=1)

    cq.wait_recv()
    for i in range(n_query):
        lo = rows_t + i * seq
        total = part[lo:lo + seq] + other[own_t * seq + i * seq:own_t * seq + (i + 1) * seq]
        q_all[d, i * half:(i + 1) * half] = gradient(total, lq_ref[i])
    qs = []
    for k in range(1, n_dp):
        c = pltpu.make_async_remote_copy(
            src_ref=q_all.at[d], dst_ref=q_all.at[d],
            send_sem=q_send.at[k], recv_sem=q_recv.at[d],
            device_id={"dp": lax.rem(d + k, n_dp)}, device_id_type=MESH,
        )
        c.start()
        qs.append(c)
    ct.wait_recv()
    for i in range(own_t):
        total = part[pl.ds(mine + i * seq, seq)] + other[i * seq:(i + 1) * seq]
        t_grad[i * half:(i + 1) * half] = gradient(total, lt_ref[core * own_t + i])

    for k in range(1, n_dp):
        src = lax.rem(d + k, n_dp)
        blk = q_all.at[src]
        pltpu.make_async_remote_copy(
            src_ref=blk, dst_ref=blk, send_sem=q_send.at[k], recv_sem=q_recv.at[src],
            device_id={"dp": src}, device_id_type=MESH,
        ).wait_recv()

    width = own_t * half
    queries = n_dp * n_query
    q_flat = q_all[...].reshape(queries * half, 2 * rank)
    pairs = lax.dot_general(q_flat, t_grad[...], NT, preferred_element_type=F32)
    pairs = pairs.reshape(queries, half, width)
    row = lax.broadcasted_iota(jnp.int32, (queries, half, width), 1)
    col = lax.broadcasted_iota(jnp.int32, (queries, half, width), 2) % half
    diag = jnp.sum(jnp.where(row == col, pairs, 0.0), axis=1)
    pick = (
        lax.broadcasted_iota(jnp.int32, (own_t, width), 1) // half
        == lax.broadcasted_iota(jnp.int32, (own_t, width), 0)
    ).astype(F32)
    out_ref[...] = lax.dot_general(
        pick, diag, NT, preferred_element_type=F32, precision=lax.Precision.HIGHEST
    )

    for c in sends + xs + ys + [cq, ct] + qs:
        c.wait_send()

    @pl.when(inside)
    def _():
        for c in inner:
            c.wait_send()


def fused(
    train_inputs, train_grads, train_lengths, query_inputs, query_grads, query_lengths,
    proj_in, proj_out,
):
    n_dp = lax.axis_size("dp")
    n_train, seq, win = train_inputs.shape
    n_query, _, wout = query_grads.shape
    _, rank, cin = proj_in.shape
    cout = proj_out.shape[2]
    rows_t, rows_q = n_train * seq, n_query * seq
    rows = rows_t + rows_q
    half = rank // 2
    own_t = n_train // 2
    cfg = (n_train, n_query, seq, rank, cin, cout, n_dp)
    hbm = pl.BlockSpec(memory_space=pltpu.HBM)
    dma = pltpu.SemaphoreType.DMA
    return pl.pallas_call(
        functools.partial(fused_kernel, cfg),
        out_shape=jax.ShapeDtypeStruct((own_t, n_dp * n_query), F32),
        in_specs=[hbm] * 8,
        out_specs=pl.BlockSpec(memory_space=pltpu.VMEM),
        scratch_shapes=[
            pltpu.SMEM((n_train,), jnp.int32),
            pltpu.SMEM((n_query,), jnp.int32),
            pltpu.VMEM((rows, win), BF16),
            pltpu.VMEM((rows, wout), BF16),
            pltpu.VMEM((n_dp, rank, cin + cout), BF16),
            pltpu.VMEM((rows, rank), F32),
            pltpu.VMEM((rows, rank), F32),
            pltpu.VMEM((rows, 2 * rank), F32),
            pltpu.VMEM((own_t * seq + rows_q, 2 * rank), F32),
            pltpu.VMEM((n_dp, n_query * half, 2 * rank), BF16),
            pltpu.VMEM((own_t * half, 2 * rank), BF16),
            dma((6,)),
            dma((2,)),
            dma((10,)),
            dma((8,)),
            dma((4,)),
            dma((4,)),
            dma((4,)),
            dma((4,)),
            dma((2,)),
            dma((2,)),
            dma((n_dp,)),
            dma((n_dp,)),
        ],
        compiler_params=pltpu.CompilerParams(
            collective_id=0, has_side_effects=True, vmem_limit_bytes=64 * 1024 * 1024
        ),
    )(
        train_inputs.reshape(rows_t, win),
        train_grads.reshape(rows_t, wout),
        train_lengths,
        query_inputs.reshape(rows_q, win),
        query_grads.reshape(rows_q, wout),
        query_lengths,
        proj_in[0],
        proj_out[0],
    )


def per_device(*args):
    proj_in, proj_out = args[6], args[7]
    sizes = (lax.axis_size("groups"), lax.axis_size("dp"), lax.axis_size("tensor"))
    fits = (
        sizes == (2, 8, 2)
        and proj_in.shape[2] % 128 == 0
        and proj_out.shape[2] % 128 == 0
        and proj_in.shape[1] == 64
        and args[0].shape[0] % 2 == 0
        and args[0].shape[1] % 16 == 0
    )
    return fused(*args) if fits else any_mesh(*args)


def solution(mesh):
    return jax.shard_map(
        per_device,
        mesh=mesh,
        in_specs=(
            P(("groups", "dp"), None, "tensor"),
            P(("groups", "dp"), None, "tensor"),
            P(("groups", "dp")),
            P(("groups", "dp"), None, "tensor"),
            P(("groups", "dp"), None, "tensor"),
            P(("groups", "dp")),
            P("tensor", None, "dp"),
            P("tensor", None, "dp"),
        ),
        out_specs=P(("groups", "dp", "tensor"), None),
        check_vma=False,
    )
```

```python
import functools

import jax
import jax.numpy as jnp
from jax import lax
from jax.experimental import pallas as pl
from jax.experimental.pallas import tpu as pltpu
from jax.sharding import PartitionSpec as P

MESH = pl.DeviceIdType.MESH
F32 = jnp.float32
BF16 = jnp.bfloat16


def project_tokens(inputs, grads, proj_in, proj_out):
    count = inputs.shape[0] * inputs.shape[1]
    in_side = lax.dot_general(
        inputs.reshape(count, inputs.shape[2]),
        proj_in,
        (((1,), (1,)), ((), ())),
        preferred_element_type=jnp.float32,
    )
    out_side = lax.dot_general(
        grads.reshape(count, grads.shape[2]),
        proj_out,
        (((1,), (1,)), ((), ())),
        preferred_element_type=jnp.float32,
    )
    joined = jnp.concatenate([in_side, out_side], axis=1)
    return joined.reshape(inputs.shape[0], inputs.shape[1], joined.shape[1])


def seq_gradient(projected, lengths, row_count):
    proj_rank = projected.shape[2] // 2
    seq_len = projected.shape[1]
    live_weight = (jnp.arange(seq_len, dtype=jnp.int32)[None, :] < lengths[:, None]).astype(
        jnp.float32
    ) / lengths.astype(jnp.float32)[:, None]
    left_side = projected[:, :, :proj_rank] * live_weight[:, :, None]
    right_side = projected[:, :, proj_rank:]
    outer = jnp.einsum("nsr,nsc->nrc", left_side, right_side)
    return outer.reshape(projected.shape[0], row_count * proj_rank).astype(jnp.bfloat16)


def pair_scores(train_grad, block):
    return lax.dot_general(
        train_grad, block, (((1,), (1,)), ((), ())), preferred_element_type=jnp.float32
    )


def score_against(train_grad, query_grad):
    return pair_scores(train_grad, lax.all_gather(query_grad, "dp", axis=0, tiled=True))


def any_mesh(
    train_inputs,
    train_grads,
    train_lengths,
    query_inputs,
    query_grads,
    query_lengths,
    proj_in,
    proj_out,
):
    whole_in, whole_out = (
        lax.all_gather(proj_in, "dp", axis=2, tiled=True),
        lax.all_gather(proj_out, "dp", axis=2, tiled=True),
    )
    half_in = whole_in[0]
    half_out = whole_out[0]
    train_part = project_tokens(train_inputs, train_grads, half_in, half_out)
    query_part = project_tokens(query_inputs, query_grads, half_in, half_out)
    proj_rank = half_in.shape[0]
    share_rows = train_inputs.shape[0] // lax.axis_size("tensor")
    core_index = lax.axis_index("tensor")
    own_lengths = lax.dynamic_slice_in_dim(train_lengths, core_index * share_rows, share_rows, 0)
    train_proj, query_proj = lax.psum((train_part, query_part), "tensor")
    own_proj = lax.dynamic_slice_in_dim(train_proj, core_index * share_rows, share_rows, 0)
    query_grad = seq_gradient(query_proj, query_lengths, proj_rank)
    return score_against(seq_gradient(own_proj, own_lengths, proj_rank), query_grad)


NT = (((1,), (1,)), ((), ()))
TN = (((0,), (0,)), ((), ()))


def fused_kernel(
    cfg,
    xt_hbm, gt_hbm, lt_hbm, xq_hbm, gq_hbm, lq_hbm, pin_hbm, pout_hbm,
    out_ref,
    lt_ref, lq_ref, x_all, g_all, p_all, acc_a, acc_b, part, other, q_all, t_grad,
    load_sem, own_sem, z_send, z_recv, x_send, x_recv, y_send, y_recv,
    c_send, c_recv, q_send, q_recv,
):
    n_train, n_query, seq, rank, cin, cout, n_dp = cfg
    n_z = n_dp // 2
    rows_t, rows_q = n_train * seq, n_query * seq
    half, quarter = rank // 2, rank // 4
    own_t = n_train // 2

    g = lax.axis_index("groups")
    d = lax.axis_index("dp")
    core = lax.axis_index("tensor")
    z, x = d // 2, d % 2

    own = [
        pltpu.make_async_copy(pin_hbm, p_all.at[d, :, pl.ds(0, cin)], own_sem.at[0]),
        pltpu.make_async_copy(pout_hbm, p_all.at[d, :, pl.ds(cin, cout)], own_sem.at[1]),
    ]
    loads = [
        pltpu.make_async_copy(xt_hbm, x_all.at[pl.ds(0, rows_t)], load_sem.at[0]),
        pltpu.make_async_copy(gt_hbm, g_all.at[pl.ds(0, rows_t)], load_sem.at[1]),
        pltpu.make_async_copy(xq_hbm, x_all.at[pl.ds(rows_t, rows_q)], load_sem.at[2]),
        pltpu.make_async_copy(gq_hbm, g_all.at[pl.ds(rows_t, rows_q)], load_sem.at[3]),
        pltpu.make_async_copy(lt_hbm, lt_ref, load_sem.at[4]),
        pltpu.make_async_copy(lq_hbm, lq_ref, load_sem.at[5]),
    ]
    for c in own:
        c.start()

    up = z // 2
    m = z + up * (n_z - 1 - 2 * z)

    def mirror(v):
        return v + up * (n_z - 1 - 2 * v)

    first = mirror(1 - m)
    inside = m == 1

    barrier = pltpu.get_barrier_semaphore()
    pl.semaphore_signal(
        barrier, inc=1, device_id={"dp": first * 2 + x}, device_id_type=MESH
    )

    @pl.when(inside)
    def _():
        pl.semaphore_signal(
            barrier, inc=1, device_id={"dp": mirror(2) * 2 + x}, device_id_type=MESH
        )

    pl.semaphore_signal(barrier, inc=1, device_id={"dp": z * 2 + 1 - x}, device_id_type=MESH)
    pl.semaphore_signal(barrier, inc=1, device_id={"tensor": 1 - core}, device_id_type=MESH)
    pl.semaphore_signal(barrier, inc=1, device_id={"groups": 1 - g}, device_id_type=MESH)
    for c in own:
        c.wait()
    for c in loads:
        c.start()
    pl.semaphore_wait(barrier, 4 + m)

    def z_copy(zb, zt, part_no, lane):
        rows = (g if part_no == 0 else 1 - g) * half
        blk = p_all.at[zb * 2 + x, pl.ds(rows, half)]
        return pltpu.make_async_remote_copy(
            src_ref=blk, dst_ref=blk,
            send_sem=z_send.at[2 * lane + part_no], recv_sem=z_recv.at[2 * zb + part_no],
            device_id={"dp": zt * 2 + x}, device_id_type=MESH,
        )

    def x_copy(zb, src_x, piece):
        blk = p_all.at[zb * 2 + src_x, pl.ds(g * half + piece * quarter, quarter)]
        return pltpu.make_async_remote_copy(
            src_ref=blk, dst_ref=blk, send_sem=x_send.at[2 * zb + piece], recv_sem=x_recv.at[2 * zb + piece],
            device_id={"dp": z * 2 + 1 - x}, device_id_type=MESH,
        )

    def y_copy(zb, src_g, piece):
        blk = p_all.at[zb * 2 + 1 - x, pl.ds(src_g * half + piece * quarter, quarter)]
        return pltpu.make_async_remote_copy(
            src_ref=blk, dst_ref=blk, send_sem=y_send.at[2 * zb + piece], recv_sem=y_recv.at[2 * zb + piece],
            device_id={"groups": 1 - g}, device_id_type=MESH,
        )

    zbs = [mirror(1 - m), mirror(2), mirror(3)]
    hops = [mirror(2), mirror(0), mirror(0)]

    sends, inner, xs, ys = [], [], [], []

    def send_inner(copy):
        inner.append(copy)

        @pl.when(inside)
        def _():
            copy.start()

    def send_x(zb):
        for piece in range(2):
            c = x_copy(zb, x, piece)
            c.start()
            xs.append(c)

    def send_own(part_no):
        c = z_copy(z, first, part_no, 0)
        c.start()
        sends.append(c)
        send_inner(z_copy(z, mirror(2), part_no, 1))

    send_own(0)
    send_x(z)

    def dots(block, start):
        cols_in = pl.ds(pl.multiple_of(block * cin, 128), cin)
        cols_out = pl.ds(pl.multiple_of(block * cout, 128), cout)
        a = lax.dot_general(
            x_all[:, cols_in], p_all[block, :, 0:cin], NT, preferred_element_type=F32
        )
        b = lax.dot_general(
            g_all[:, cols_out], p_all[block, :, cin:cin + cout], NT, preferred_element_type=F32
        )
        if start:
            acc_a[...] = a
            acc_b[...] = b
        else:
            acc_a[...] += a
            acc_b[...] += b

    order = [z] + zbs

    def hand_on(k):
        for piece in range(2):
            x_copy(order[k], 1 - x, piece).wait_recv()
            c = y_copy(order[k], g, piece)
            c.start()
            ys.append(c)

    def finish(k):
        for piece in range(2):
            y_copy(order[k], 1 - g, piece).wait_recv()
        dots(order[k] * 2 + 1 - x, False)

    for k in range(n_z - 1):
        zb = zbs[k]
        z_copy(zb, first, 0, 0).wait_recv()
        send_inner(z_copy(zb, hops[k], 0, 2 + k))
        send_x(zb)
        if k == 0:
            send_own(1)
        hand_on(k)
        if k == 0:
            for c in loads:
                c.wait()
            dots(d, True)
    finish(0)
    for k in range(n_z - 1):
        zb = zbs[k]
        z_copy(zb, first, 1, 0).wait_recv()
        send_inner(z_copy(zb, hops[k], 1, 2 + k))
        if k == 0:
            hand_on(n_z - 1)
        dots(zb * 2 + x, False)
        finish(k + 1)

    part[:, 0:rank] = acc_a[...]
    part[:, rank:2 * rank] = acc_b[...]

    mine = core * (own_t * seq)
    theirs = (1 - core) * (own_t * seq)
    cq = pltpu.make_async_remote_copy(
        src_ref=part.at[pl.ds(rows_t, rows_q)], dst_ref=other.at[pl.ds(own_t * seq, rows_q)],
        send_sem=c_send.at[0], recv_sem=c_recv.at[0],
        device_id={"tensor": 1 - core}, device_id_type=MESH,
    )
    ct = pltpu.make_async_remote_copy(
        src_ref=part.at[pl.ds(theirs, own_t * seq)], dst_ref=other.at[pl.ds(0, own_t * seq)],
        send_sem=c_send.at[1], recv_sem=c_recv.at[1],
        device_id={"tensor": 1 - core}, device_id_type=MESH,
    )
    cq.start()
    ct.start()

    step = lax.broadcasted_iota(jnp.int32, (seq, rank), 0)

    def gradient(total, length):
        size = jnp.broadcast_to(length, (seq, rank))
        weight = jnp.where(step < size, 1.0, 0.0) / size.astype(F32)
        a = total[:, 0:rank] * weight
        b = total[:, rank:2 * rank]
        h = lax.dot_general(
            a, b, TN, preferred_element_type=F32, precision=lax.Precision.HIGHEST
        ).astype(BF16)
        return jnp.concatenate([h[0:half], h[half:rank]], axis=1)

    cq.wait_recv()
    for i in range(n_query):
        lo = rows_t + i * seq
        total = part[lo:lo + seq] + other[own_t * seq + i * seq:own_t * seq + (i + 1) * seq]
        q_all[d, i * half:(i + 1) * half] = gradient(total, lq_ref[i])
    qs = []
    for k in range(1, n_dp):
        c = pltpu.make_async_remote_copy(
            src_ref=q_all.at[d], dst_ref=q_all.at[d],
            send_sem=q_send.at[k], recv_sem=q_recv.at[d],
            device_id={"dp": lax.rem(d + k, n_dp)}, device_id_type=MESH,
        )
        c.start()
        qs.append(c)
    ct.wait_recv()
    for i in range(own_t):
        total = part[pl.ds(mine + i * seq, seq)] + other[i * seq:(i + 1) * seq]
        t_grad[i * half:(i + 1) * half] = gradient(total, lt_ref[core * own_t + i])

    for k in range(1, n_dp):
        src = lax.rem(d + k, n_dp)
        blk = q_all.at[src]
        pltpu.make_async_remote_copy(
            src_ref=blk, dst_ref=blk, send_sem=q_send.at[k], recv_sem=q_recv.at[src],
            device_id={"dp": src}, device_id_type=MESH,
        ).wait_recv()

    width = own_t * half
    queries = n_dp * n_query
    q_flat = q_all[...].reshape(queries * half, 2 * rank)
    pairs = lax.dot_general(q_flat, t_grad[...], NT, preferred_element_type=F32)
    pairs = pairs.reshape(queries, half, width)
    row = lax.broadcasted_iota(jnp.int32, (queries, half, width), 1)
    col = lax.broadcasted_iota(jnp.int32, (queries, half, width), 2) % half
    diag = jnp.sum(jnp.where(row == col, pairs, 0.0), axis=1)
    pick = (
        lax.broadcasted_iota(jnp.int32, (own_t, width), 1) // half
        == lax.broadcasted_iota(jnp.int32, (own_t, width), 0)
    ).astype(F32)
    out_ref[...] = lax.dot_general(
        pick, diag, NT, preferred_element_type=F32, precision=lax.Precision.HIGHEST
    )

    for c in sends + xs + ys + [cq, ct] + qs:
        c.wait_send()

    @pl.when(inside)
    def _():
        for c in inner:
            c.wait_send()


def fused(
    train_inputs, train_grads, train_lengths, query_inputs, query_grads, query_lengths,
    proj_in, proj_out,
):
    n_dp = lax.axis_size("dp")
    n_train, seq, win = train_inputs.shape
    n_query, _, wout = query_grads.shape
    _, rank, cin = proj_in.shape
    cout = proj_out.shape[2]
    rows_t, rows_q = n_train * seq, n_query * seq
    rows = rows_t + rows_q
    half = rank // 2
    own_t = n_train // 2
    cfg = (n_train, n_query, seq, rank, cin, cout, n_dp)
    hbm = pl.BlockSpec(memory_space=pltpu.HBM)
    dma = pltpu.SemaphoreType.DMA
    return pl.pallas_call(
        functools.partial(fused_kernel, cfg),
        out_shape=jax.ShapeDtypeStruct((own_t, n_dp * n_query), F32),
        in_specs=[hbm] * 8,
        out_specs=pl.BlockSpec(memory_space=pltpu.VMEM),
        scratch_shapes=[
            pltpu.SMEM((n_train,), jnp.int32),
            pltpu.SMEM((n_query,), jnp.int32),
            pltpu.VMEM((rows, win), BF16),
            pltpu.VMEM((rows, wout), BF16),
            pltpu.VMEM((n_dp, rank, cin + cout), BF16),
            pltpu.VMEM((rows, rank), F32),
            pltpu.VMEM((rows, rank), F32),
            pltpu.VMEM((rows, 2 * rank), F32),
            pltpu.VMEM((own_t * seq + rows_q, 2 * rank), F32),
            pltpu.VMEM((n_dp, n_query * half, 2 * rank), BF16),
            pltpu.VMEM((own_t * half, 2 * rank), BF16),
            dma((6,)),
            dma((2,)),
            dma((10,)),
            dma((8,)),
            dma((8,)),
            dma((8,)),
            dma((9,)),
            dma((9,)),
            dma((2,)),
            dma((2,)),
            dma((n_dp,)),
            dma((n_dp,)),
        ],
        compiler_params=pltpu.CompilerParams(
            collective_id=0, has_side_effects=True, vmem_limit_bytes=64 * 1024 * 1024
        ),
    )(
        train_inputs.reshape(rows_t, win),
        train_grads.reshape(rows_t, wout),
        train_lengths,
        query_inputs.reshape(rows_q, win),
        query_grads.reshape(rows_q, wout),
        query_lengths,
        proj_in[0],
        proj_out[0],
    )


def per_device(*args):
    proj_in, proj_out = args[6], args[7]
    sizes = (lax.axis_size("groups"), lax.axis_size("dp"), lax.axis_size("tensor"))
    fits = (
        sizes == (2, 8, 2)
        and proj_in.shape[2] % 128 == 0
        and proj_out.shape[2] % 128 == 0
        and proj_in.shape[1] == 64
        and args[0].shape[0] % 2 == 0
        and args[0].shape[1] % 16 == 0
    )
    return fused(*args) if fits else any_mesh(*args)


def solution(mesh):
    return jax.shard_map(
        per_device,
        mesh=mesh,
        in_specs=(
            P(("groups", "dp"), None, "tensor"),
            P(("groups", "dp"), None, "tensor"),
            P(("groups", "dp")),
            P(("groups", "dp"), None, "tensor"),
            P(("groups", "dp"), None, "tensor"),
            P(("groups", "dp")),
            P("tensor", None, "dp"),
            P("tensor", None, "dp"),
        ),
        out_specs=P(("groups", "dp", "tensor"), None),
        check_vma=False,
    )
```
